32 devices in a mesh: dp: 8 (over y, x, core), mp: 4 (over z).
Axes of the slice: x: 2, y: 2, z: 4, core: 2. Of those that a mesh axis runs over, the one named last changes fastest.
Arguments:
- query_rows: bfloat16 [2048, 5120], P('dp', 'mp'), may hold values from -160 to 160
- key_rows: bfloat16 [2048, 1024], P('dp', 'mp'), may hold values from -8 to 8
- value_rows: bfloat16 [2048, 1024], P('dp', 'mp'), may hold values from -6 to 6
- grad_out: bfloat16 [2048, 5120], P('dp', 'mp'), may hold values from -6 to 6
- out_proj: bfloat16 [5120, 5120], P('mp'), may hold values from -0.078125 to 0.078125
- lengths: int32 [32, 4], replicated, may hold values from 1 to 48, 64 in all within a row
- offsets: int32 [4], replicated, may hold values from 0 to 7, as said below
Outputs:
- grad_query: bfloat16 [2048, 5120], P('dp', 'mp')
- grad_key: bfloat16 [2048, 1024], P('dp', 'mp')
- grad_value: bfloat16 [2048, 1024], P('dp', 'mp')
- grad_proj: float32 [5120, 5120], P('dp', 'mp')
The draws below stay inside these ranges and needn't reach their ends.
Inputs may be any that keep to these rules, and one draw needn't show every extreme that they name: Each row is the document lengths of one block, summing to 64; the longest is exactly 48. `offsets`: the 4 values are distinct.
All inputs are finite; a program needn't handle non-finite values.
Results may differ from the reference program's by a relative error of at most 0.033.
Values may be sent and summed in bfloat16 or wider, within the bound.
A program may use at most 128 MiB of HBM per device.

```python
import math
import jax
import jax.numpy as jnp
import numpy as np
from jax import lax

D = 5120
HEADS = 40
KVH = 8
HD = 128
BLOCK = 64
NCH = 4
NDOC = 4
MOST = 48
NCHUNKS = 32
TOKENS = 2048
N_DP = 8


def joint_draw(key):
    base = jax.random.fold_in(key, 4242)
    first, second = jax.random.split(base, 2)
    key_vals = jax.random.truncated_normal(first, -6.0, 6.0, (TOKENS, KVH * HD), jnp.float32)
    query_vals = jax.random.truncated_normal(second, -6.0, 6.0, (TOKENS, HEADS * HD), jnp.float32)
    return (query_vals, key_vals)


def draw_query_rows(key, part):
    query_vals, key_vals = joint_draw(key)
    return query_vals.astype(jnp.bfloat16)


def draw_key_rows(key, part):
    query_vals, key_vals = joint_draw(key)
    return key_vals.astype(jnp.bfloat16)


def draw_offsets(key, part):
    middle = (jax.random.permutation(jax.random.fold_in(key, 99), N_DP - 2) + 1).astype(jnp.int32)
    listed = jnp.concatenate([jnp.full((1,), N_DP - 1, jnp.int32), jnp.zeros((1,), jnp.int32), middle])
    picks = listed[:NCH]
    order = jax.random.permutation(jax.random.fold_in(key, 98), NCH)
    return picks[order].astype(jnp.int32)


def raised(array, key, source, target, blocks, factor):
    owner, partner = [(jnp.arange(array.shape[dim]) // (array.shape[dim] // blocks)).reshape([-1 if axis == dim else 1 for axis in range(array.ndim)]) for dim in (source, target)]
    chosen = jax.random.permutation(key, blocks)[partner]
    strong = (owner == chosen) | (owner == (partner + blocks // 2) % blocks)
    return jnp.where(strong, factor * array, array)


def steps_of(stream_key, dims, shards, least, top_value):
    factor_of = 1.0
    for dim, blocks in shards:
        steps = jax.random.uniform(jax.random.fold_in(jax.random.fold_in(stream_key, 6), dim), (blocks,), jnp.float32, least / len(shards), top_value / len(shards))
        factor_of = factor_of * jnp.repeat(jnp.exp(steps), dims[dim] // blocks).reshape((-1,) + (1,) * (len(dims) - 1 - dim))
    return factor_of


def split_up(amount, total, bound, skew):
    portions = [(1 << 20) // math.isqrt(standing ** skew) + 1 for standing in range(2, amount + 1)]
    surplus, counts = total - bound - (amount - 1), [1] * (amount - 1)
    while surplus > 0:
        candidates = [i for i in range(amount - 1) if counts[i] < bound]
        whole, budget = sum([portions[i] for i in candidates]), surplus
        for i in candidates:
            extra = min(bound - counts[i], max(1, budget * portions[i] // whole), surplus)
            counts[i] = counts[i] + extra
            surplus = surplus - extra
    return np.array([bound] + counts)


def uneven(stream_key, amount, total, bound, skew):
    if amount == 2:
        one = jax.random.randint(stream_key, (), max(1, total - bound), min(bound, total - 1) + 1)
        return jnp.stack([one, total - one])
    tallies = jnp.asarray(split_up(amount, total, bound, skew), jnp.int32)
    pairs = (amount - 1) // 2
    donor, receiver = tallies[1:1 + 2 * pairs:2], tallies[2:2 + 2 * pairs:2]
    slack = jnp.minimum(donor - 1, bound - receiver)
    moved = jax.random.randint(jax.random.fold_in(stream_key, 1), (pairs,), 0, 1 << 20) % (slack + 1)
    tallies = tallies.at[1:1 + 2 * pairs:2].set(donor - moved).at[2:2 + 2 * pairs:2].set(receiver + moved)
    return tallies[jax.random.permutation(jax.random.fold_in(stream_key, 2), amount)]


def noise(stream_key, extent, spread, most, cuts=(), kind=jnp.bfloat16):
    entries = spread * jax.random.normal(stream_key, extent, jnp.float32)
    if cuts:
        entries = entries * steps_of(stream_key, extent, cuts, -0.22, 0.18)
    return jnp.clip(entries, -most, most).astype(kind)


def heavy_noise(stream_key, dims, spread, bound, pieces, heavy, kind=jnp.bfloat16):
    drawn = spread * jax.random.normal(stream_key, dims, jnp.float32)
    if pieces:
        drawn = drawn * steps_of(stream_key, dims, pieces, -0.22, 0.18)
    return jnp.clip(raised(drawn, jax.random.fold_in(stream_key, 3), *heavy), -bound, bound).astype(kind)


def setup_inputs(seed: int = 0) -> dict:
    splits = jax.random.split(jax.random.key(seed), 8)
    query_rows = draw_query_rows(jax.random.fold_in(splits[7], 71), 0)
    key_rows = draw_key_rows(jax.random.fold_in(splits[7], 71), 0)
    value_rows = noise(splits[2], (TOKENS, KVH * HD), 1.0, 6.0, ((0, 8), (1, 4)))
    grad_out = heavy_noise(splits[3], (TOKENS, D), 1.0, 6.0, ((0, 8), (1, 4)), (0, 1, 8, 2.0))
    out_proj = noise(splits[4], (HEADS * HD, D), (HEADS * HD) ** -0.5, 0.078125, ((0, 4),))
    lengths = jax.vmap(lambda own: uneven(own, NDOC, BLOCK, MOST, 2))(jax.random.split(splits[5], NCHUNKS)).reshape((NCHUNKS, NDOC)).astype(jnp.int32)
    offsets = draw_offsets(jax.random.fold_in(splits[7], 71), 0)
    return {"query_rows": query_rows, "key_rows": key_rows, "value_rows": value_rows, "grad_out": grad_out, "out_proj": out_proj, "lengths": lengths, "offsets": offsets}


def doc_layout(lengths, block_len):
    doc_ends = jnp.cumsum(lengths, axis=1).astype(jnp.int32)
    positions = jnp.arange(block_len, dtype=jnp.int32)
    segment = jnp.sum((doc_ends[:, None, :] <= positions[None, :, None]).astype(jnp.int32), axis=2).astype(jnp.int32)
    doc_ids = jnp.arange(lengths.shape[1], dtype=jnp.int32)
    onehot_doc = segment[:, :, None] == doc_ids[None, None, :]
    own_length = jnp.sum(jnp.where(onehot_doc, lengths[:, None, :], 0), axis=2)
    token_weight = 1.0 / own_length.astype(jnp.float32)
    return segment, token_weight


def block_grads(query_blk, key_blk, value_blk, grad_blk, segment):
    length = query_blk.shape[0]
    scaling = query_blk.shape[-1] ** -0.5
    positions = jnp.arange(length, dtype=jnp.int32)
    allowed = (segment[:, None] == segment[None, :]) & (positions[None, :] <= positions[:, None])
    query_float = query_blk.astype(jnp.float32)
    key_float = key_blk.astype(jnp.float32)
    value_float = value_blk.astype(jnp.float32)
    grad_float = grad_blk.astype(jnp.float32)
    scores = jnp.einsum("qkgd,pkd->kgqp", query_float, key_float) * scaling
    scores = jnp.where(allowed[None, None], scores, -1e30)
    top_score = jnp.max(scores, axis=-1, keepdims=True)
    exponent = jnp.where(allowed[None, None], jnp.exp(scores - top_score), 0.0)
    denominator = jnp.sum(exponent, axis=-1, keepdims=True)
    soft = exponent / denominator
    soft_weight = soft.astype(jnp.bfloat16)
    attended = jnp.einsum("kgqp,pkd->qkgd", soft_weight.astype(jnp.float32), value_float).astype(jnp.bfloat16)
    row_dot = jnp.sum(grad_float * attended.astype(jnp.float32), axis=-1)
    grad_soft = jnp.einsum("qkgd,pkd->kgqp", grad_float, value_float)
    grad_score = (soft * (grad_soft - jnp.transpose(row_dot, (1, 2, 0))[..., None])).astype(jnp.bfloat16)
    score_float = grad_score.astype(jnp.float32)
    grad_q = (jnp.einsum("kgqp,pkd->qkgd", score_float, key_float) * scaling).astype(jnp.bfloat16)
    grad_k = (jnp.einsum("kgqp,qkgd->pkd", score_float, query_float) * scaling).astype(jnp.bfloat16)
    grad_v = jnp.einsum("kgqp,qkgd->pkd", soft_weight.astype(jnp.float32), grad_float).astype(jnp.bfloat16)
    return attended, grad_q, grad_k, grad_v


def reference(query_rows, key_rows, value_rows, grad_out, out_proj, lengths, offsets):
    segment, token_weight = doc_layout(lengths, BLOCK)
    weighted = (grad_out.astype(jnp.float32) * token_weight.reshape(-1, 1)).astype(jnp.bfloat16)
    head_grad = lax.dot_general(weighted, out_proj, (((1,), (1,)), ((), ())), preferred_element_type=jnp.float32).astype(jnp.bfloat16)
    ranks = jnp.arange(N_DP, dtype=jnp.int32)
    slot_ids = jnp.arange(NCH, dtype=jnp.int32)
    sources = ((((ranks[:, None] - offsets[None, :]) % N_DP) * NCH) + slot_ids[None, :]).reshape(-1).astype(jnp.int32)
    group = HEADS // KVH

    def moved(matrix):
        return matrix.reshape(NCHUNKS, BLOCK, matrix.shape[1])[sources]

    query_moved = moved(query_rows).reshape(NCHUNKS, BLOCK, KVH, group, HD)
    key_moved = moved(key_rows).reshape(NCHUNKS, BLOCK, KVH, HD)
    value_moved = moved(value_rows).reshape(NCHUNKS, BLOCK, KVH, HD)
    grad_moved = moved(head_grad).reshape(NCHUNKS, BLOCK, KVH, group, HD)
    segment_moved = segment[sources]

    def one_block(items):
        return block_grads(items[0], items[1], items[2], items[3], items[4])

    attended, grad_q, grad_k, grad_v = lax.map(one_block, (query_moved, key_moved, value_moved, grad_moved, segment_moved))
    weighted_moved = moved(weighted).reshape(TOKENS, D)
    grad_proj = lax.dot_general(weighted_moved, attended.reshape(TOKENS, HEADS * HD), (((0,), (0,)), ((), ())), preferred_element_type=jnp.float32)
    return (grad_q.reshape(TOKENS, HEADS * HD), grad_k.reshape(TOKENS, KVH * HD), grad_v.reshape(TOKENS, KVH * HD), grad_proj)
```

```python
import jax
import jax.numpy as jnp
from jax import lax
from jax.sharding import PartitionSpec as P

HEADS = 40
KVH = 8
HD = 128


def doc_layout(lengths, block_len):
    doc_ends = jnp.cumsum(lengths, axis=1)
    positions = jnp.arange(block_len, dtype=jnp.int32)
    segment = jnp.sum((doc_ends[:, None, :] <= positions[None, :, None]).astype(jnp.int32), axis=2)
    doc_ids = jnp.arange(lengths.shape[1], dtype=jnp.int32)
    onehot_doc = segment[:, :, None] == doc_ids[None, None, :]
    own_length = jnp.sum(jnp.where(onehot_doc, lengths[:, None, :], 0), axis=2)
    token_weight = 1.0 / own_length.astype(jnp.float32)
    return (segment, token_weight)


def block_grads(query_blk, key_blk, value_blk, grad_blk, segment):
    length = query_blk.shape[0]
    scaling = query_blk.shape[-1] ** (-0.5)
    positions = jnp.arange(length, dtype=jnp.int32)
    allowed = (segment[:, None] == segment[None, :]) & (positions[None, :] <= positions[:, None])
    scores = (
        jnp.einsum("qkgd,pkd->kgqp", query_blk, key_blk, preferred_element_type=jnp.float32)
        * scaling
    )
    scores = jnp.where(allowed[None, None], scores, -1e30)
    top_score = jnp.max(scores, axis=-1, keepdims=True)
    exponent = jnp.where(allowed[None, None], jnp.exp(scores - top_score), 0.0)
    denominator = jnp.sum(exponent, axis=-1, keepdims=True)
    soft = exponent / denominator
    soft_weight = soft.astype(jnp.bfloat16)
    attended = jnp.einsum(
        "kgqp,pkd->qkgd", soft_weight, value_blk, preferred_element_type=jnp.float32
    ).astype(jnp.bfloat16)
    row_dot = jnp.sum(grad_blk.astype(jnp.float32) * attended.astype(jnp.float32), axis=-1)
    grad_soft = jnp.einsum(
        "qkgd,pkd->kgqp", grad_blk, value_blk, preferred_element_type=jnp.float32
    )
    grad_score = (soft * (grad_soft - jnp.transpose(row_dot, (1, 2, 0))[..., None])).astype(
        jnp.bfloat16
    )
    grad_q = (
        jnp.einsum("kgqp,pkd->qkgd", grad_score, key_blk, preferred_element_type=jnp.float32)
        * scaling
    ).astype(jnp.bfloat16)
    grad_k = (
        jnp.einsum("kgqp,qkgd->pkd", grad_score, query_blk, preferred_element_type=jnp.float32)
        * scaling
    ).astype(jnp.bfloat16)
    grad_v = jnp.einsum(
        "kgqp,qkgd->pkd", soft_weight, grad_blk, preferred_element_type=jnp.float32
    ).astype(jnp.bfloat16)
    return (attended, grad_q, grad_k, grad_v)


def local(query_rows, key_rows, value_rows, grad_out, out_proj, lengths, offsets):
    data_ranks = lax.axis_size("dp")
    my_rank = lax.axis_index("dp")
    slot_count = offsets.shape[0]
    tokens_here = query_rows.shape[0]
    block_len = tokens_here // slot_count
    slot_ids = jnp.arange(slot_count, dtype=jnp.int32)
    peer_ids = jnp.arange(data_ranks, dtype=jnp.int32)
    targets = (my_rank + offsets) % data_ranks
    sources = (my_rank - offsets) % data_ranks
    home_lengths = lax.dynamic_slice_in_dim(lengths, my_rank * slot_count, slot_count, 0)
    segment, weight = doc_layout(home_lengths, block_len)
    weighted = (grad_out.astype(jnp.float32) * weight.reshape(-1, 1)).astype(jnp.bfloat16)
    group = HEADS // KVH
    features = query_rows.shape[1]
    kv_local = key_rows.shape[1] // HD

    whole_cot = lax.all_gather(weighted, "mp", axis=1, tiled=True)
    width = whole_cot.shape[1]
    gather = data_ranks * tokens_here * (features + width // data_ranks) < width * features
    if gather:
        cot_cols = lax.all_to_all(whole_cot, "dp", split_axis=1, concat_axis=0, tiled=True)
    head_grad = lax.dot_general(
        whole_cot, out_proj, (((1,), (1,)), ((), ())), preferred_element_type=jnp.float32
    ).astype(jnp.bfloat16)
    attended, grad_q, grad_k, grad_v = jax.vmap(block_grads)(
        query_rows.reshape(slot_count, block_len, kv_local, group, HD),
        key_rows.reshape(slot_count, block_len, kv_local, HD),
        value_rows.reshape(slot_count, block_len, kv_local, HD),
        head_grad.reshape(slot_count, block_len, kv_local, group, HD),
        segment,
    )
    attended_rows = attended.reshape(tokens_here, features)
    if gather:
        everyone = lax.all_gather(attended_rows, "dp", axis=0, tiled=True)
        grad_proj = lax.dot_general(
            cot_cols, everyone, (((0,), (0,)), ((), ())), preferred_element_type=jnp.float32
        )
    else:
        grad_proj = lax.psum_scatter(
            lax.dot_general(
                whole_cot, attended_rows, (((0,), (0,)), ((), ())), preferred_element_type=jnp.float32
            ),
            "dp",
            scatter_dimension=0,
            tiled=True,
        )

    grads = jnp.concatenate(
        [part.reshape(slot_count, block_len, -1) for part in (grad_q, grad_k, grad_v)], axis=2
    )
    matches = targets[None, :] == peer_ids[:, None]
    picked = jnp.sum(jnp.where(matches, slot_ids[None, :], 0), axis=1)
    filled = jnp.any(matches, axis=1)
    parcels = jnp.where(filled[:, None, None], grads[picked], jnp.zeros((), grads.dtype))
    arrived = lax.all_to_all(parcels, "dp", split_axis=0, concat_axis=0, tiled=True)
    moved = arrived[sources].reshape(tokens_here, -1)
    return (
        moved[:, :features],
        moved[:, features : features + key_rows.shape[1]],
        moved[:, features + key_rows.shape[1] :],
        grad_proj,
    )


def solution(mesh):
    return jax.shard_map(
        local,
        mesh=mesh,
        in_specs=(
            P("dp", "mp"),
            P("dp", "mp"),
            P("dp", "mp"),
            P("dp", "mp"),
            P("mp", None),
            P(),
            P(),
        ),
        out_specs=(P("dp", "mp"), P("dp", "mp"), P("dp", "mp"), P("dp", "mp")),
        check_vma=False,
    )
```

```python
import functools

import jax
import jax.numpy as jnp
from jax import lax
from jax.experimental import pallas as pl
from jax.experimental.pallas import tpu as pltpu
from jax.sharding import PartitionSpec as P

HEADS = 40
KVH = 8
HD = 128


def doc_layout(lengths, block_len):
    doc_ends = jnp.cumsum(lengths, axis=1)
    positions = jnp.arange(block_len, dtype=jnp.int32)
    segment = jnp.sum((doc_ends[:, None, :] <= positions[None, :, None]).astype(jnp.int32), axis=2)
    doc_ids = jnp.arange(lengths.shape[1], dtype=jnp.int32)
    onehot_doc = segment[:, :, None] == doc_ids[None, None, :]
    own_length = jnp.sum(jnp.where(onehot_doc, lengths[:, None, :], 0), axis=2)
    token_weight = 1.0 / own_length.astype(jnp.float32)
    return (segment, token_weight)


def block_grads(query_blk, key_blk, value_blk, grad_blk, segment):
    length = query_blk.shape[0]
    scaling = query_blk.shape[-1] ** (-0.5)
    positions = jnp.arange(length, dtype=jnp.int32)
    allowed = (segment[:, None] == segment[None, :]) & (positions[None, :] <= positions[:, None])
    scores = (
        jnp.einsum("qkgd,pkd->kgqp", query_blk, key_blk, preferred_element_type=jnp.float32)
        * scaling
    )
    scores = jnp.where(allowed[None, None], scores, -1e30)
    top_score = jnp.max(scores, axis=-1, keepdims=True)
    exponent = jnp.where(allowed[None, None], jnp.exp(scores - top_score), 0.0)
    denominator = jnp.sum(exponent, axis=-1, keepdims=True)
    soft = exponent / denominator
    soft_weight = soft.astype(jnp.bfloat16)
    attended = jnp.einsum(
        "kgqp,pkd->qkgd", soft_weight, value_blk, preferred_element_type=jnp.float32
    ).astype(jnp.bfloat16)
    row_dot = jnp.sum(grad_blk.astype(jnp.float32) * attended.astype(jnp.float32), axis=-1)
    grad_soft = jnp.einsum(
        "qkgd,pkd->kgqp", grad_blk, value_blk, preferred_element_type=jnp.float32
    )
    grad_score = (soft * (grad_soft - jnp.transpose(row_dot, (1, 2, 0))[..., None])).astype(
        jnp.bfloat16
    )
    grad_q = (
        jnp.einsum("kgqp,pkd->qkgd", grad_score, key_blk, preferred_element_type=jnp.float32)
        * scaling
    ).astype(jnp.bfloat16)
    grad_k = (
        jnp.einsum("kgqp,qkgd->pkd", grad_score, query_blk, preferred_element_type=jnp.float32)
        * scaling
    ).astype(jnp.bfloat16)
    grad_v = jnp.einsum(
        "kgqp,qkgd->pkd", soft_weight, grad_blk, preferred_element_type=jnp.float32
    ).astype(jnp.bfloat16)
    return (attended, grad_q, grad_k, grad_v)


def push(src, dst, send, recv, **where):
    return pltpu.make_async_remote_copy(
        src_ref=src,
        dst_ref=dst,
        send_sem=send,
        recv_sem=recv,
        device_id=where,
        device_id_type=pl.DeviceIdType.MESH,
    )


def greet(axis_sizes):
    barrier = pltpu.get_barrier_semaphore()
    for axis, size in axis_sizes:
        for step in range(1, size):
            pl.semaphore_signal(
                barrier,
                inc=1,
                device_id={axis: (lax.axis_index(axis) + step) % size},
                device_id_type=pl.DeviceIdType.MESH,
            )
    pl.semaphore_wait(barrier, sum(size - 1 for _, size in axis_sizes))


CHUNKS = 2


def spread_kernel(n_dp, n_mp, own, whole, cols, own_sem, z_send, z_recv, c_send, c_recv, c_own):
    d, m = lax.axis_index("dp"), lax.axis_index("mp")
    rows, feat = own.shape
    piece = cols.shape[2]
    per = feat // piece
    part = rows // CHUNKS

    def shard(j, c):
        return whole.at[pl.ds(c * part, part), pl.ds(pl.multiple_of(j * feat, 128), feat)]

    def hop(way, s, c):
        j = m - s if way == 0 else m + s
        src = own.at[pl.ds(c * part, part), :] if s == 0 else shard(j, c)
        goal = m + 1 if way == 0 else m - 1
        return push(src, shard(j, c), z_send.at[way, s, c], z_recv.at[way, s, c], mp=goal)

    def sends(way, s):
        return (m + 1 < n_mp) & (m - s >= 0) if way == 0 else (m >= 1) & (m + s < n_mp)

    def comes(way, s):
        return m - 1 - s >= 0 if way == 0 else m + 1 + s < n_mp

    def landing(way, s, c):
        j = m - 1 - s if way == 0 else m + 1 + s
        came = m - 1 if way == 0 else m + 1
        return push(shard(j, c), shard(j, c), z_send.at[way, s, c], z_recv.at[way, s, c], mp=came)

    def pass_columns(j, mine):
        for p in range(per):
            goal = j * per + p
            if mine:
                src = own.at[:, pl.ds(p * piece, piece)]
            else:
                src = whole.at[:, pl.ds(pl.multiple_of(j * feat + p * piece, 128), piece)]

            @pl.when(goal == d)
            def _():
                pltpu.make_async_copy(src, cols.at[d], c_own).start()

            @pl.when(goal != d)
            def _():
                push(src, cols.at[d], c_send.at[goal], c_recv.at[d], dp=goal).start()

    greet((("dp", n_dp), ("mp", n_mp)))
    for c in range(CHUNKS):
        for way in range(2):

            @pl.when(sends(way, 0))
            def _():
                hop(way, 0, c).start()

    keep = pltpu.make_async_copy(
        own, whole.at[:, pl.ds(pl.multiple_of(m * feat, 128), feat)], own_sem
    )
    keep.start()
    pass_columns(m, True)
    for s in range(n_mp - 1):
        for c in range(CHUNKS):
            for way in range(2):

                @pl.when(comes(way, s))
                def _():
                    landing(way, s, c).wait_recv()
                    if s + 1 < n_mp - 1:

                        @pl.when(sends(way, s + 1))
                        def _():
                            hop(way, s + 1, c).start()

        for way in range(2):

            @pl.when(comes(way, s))
            def _():
                pass_columns(m - 1 - s if way == 0 else m + 1 + s, False)

    keep.wait()
    for s in range(n_mp - 1):
        for c in range(CHUNKS):
            for way in range(2):

                @pl.when(sends(way, s))
                def _():
                    hop(way, s, c).wait_send()

    sample = own.at[:, pl.ds(0, piece)]
    pltpu.make_async_copy(sample, cols.at[d], c_own).wait()
    for peer in range(n_dp):

        @pl.when(peer != d)
        def _():
            copy = push(sample, cols.at[peer], c_send.at[peer], c_recv.at[peer], dp=peer)
            copy.wait_send()
            copy.wait_recv()


def share_kernel(
    n_dp, own, parcels, everyone, arrived, own_sem, a_send, a_recv, f_send, f_recv, p_send, p_recv
):
    d = lax.axis_index("dp")
    chips = n_dp // 2
    chip, core = d // 2, d % 2
    mate = chip * 2 + 1 - core
    greet((("dp", n_dp),))
    for k in range(1, chips):
        goal = ((chip + k) % chips) * 2 + core
        push(own, everyone.at[d], a_send.at[k], a_recv.at[k], dp=goal).start()
    push(own, everyone.at[d], a_send.at[0], a_recv.at[0], dp=mate).start()
    for k in range(1, n_dp):
        goal = (d + k) % n_dp
        push(parcels.at[goal], arrived.at[d], p_send.at[k], p_recv.at[k], dp=goal).start()
    keeps = (
        pltpu.make_async_copy(own, everyone.at[d], own_sem.at[0]),
        pltpu.make_async_copy(parcels.at[d], arrived.at[d], own_sem.at[1]),
    )
    for keep in keeps:
        keep.start()

    def passed(k, side, goal):
        block = everyone.at[((chip + chips - k) % chips) * 2 + side]
        return push(block, block, f_send.at[k], f_recv.at[k], dp=goal)

    for k in range(1, chips):
        origin = ((chip + chips - k) % chips) * 2 + core
        push(own, everyone.at[origin], a_send.at[k], a_recv.at[k], dp=origin).wait_recv()
        passed(k, core, mate).start()
    push(own, everyone.at[mate], a_send.at[0], a_recv.at[0], dp=mate).wait_recv()
    for k in range(1, n_dp):
        origin = (d + n_dp - k) % n_dp
        copy = push(parcels.at[d], arrived.at[origin], p_send.at[k], p_recv.at[k], dp=origin)
        copy.wait_recv()
        copy.wait_send()
    for k in range(1, chips):
        passed(k, 1 - core, mate).wait_recv()
        passed(k, core, mate).wait_send()
    for k in range(chips):
        push(own, everyone.at[d], a_send.at[k], a_recv.at[k], dp=mate).wait_send()
    for keep in keeps:
        keep.wait()


def spread(weighted, n_dp, n_mp):
    rows, feat = weighted.shape
    piece = feat * n_mp // n_dp
    dma = pltpu.SemaphoreType.DMA
    anywhere = pl.BlockSpec(memory_space=pl.ANY)
    return pl.pallas_call(
        functools.partial(spread_kernel, n_dp, n_mp),
        out_shape=(
            jax.ShapeDtypeStruct((rows, feat * n_mp), weighted.dtype),
            jax.ShapeDtypeStruct((n_dp, rows, piece), weighted.dtype),
        ),
        in_specs=[anywhere],
        out_specs=(anywhere, anywhere),
        scratch_shapes=[
            dma(()),
            dma((2, n_mp - 1, CHUNKS)),
            dma((2, n_mp - 1, CHUNKS)),
            dma((n_dp,)),
            dma((n_dp,)),
            dma(()),
        ],
        compiler_params=pltpu.CompilerParams(collective_id=0, has_side_effects=True),
    )(weighted)


def share(rows, parcels, n_dp):
    dma = pltpu.SemaphoreType.DMA
    anywhere = pl.BlockSpec(memory_space=pl.ANY)
    return pl.pallas_call(
        functools.partial(share_kernel, n_dp),
        out_shape=(
            jax.ShapeDtypeStruct((n_dp, *rows.shape), rows.dtype),
            jax.ShapeDtypeStruct(parcels.shape, parcels.dtype),
        ),
        in_specs=[anywhere, anywhere],
        out_specs=(anywhere, anywhere),
        scratch_shapes=[
            dma((2,)),
            dma((n_dp // 2,)),
            dma((n_dp // 2,)),
            dma((n_dp // 2,)),
            dma((n_dp // 2,)),
            dma((n_dp,)),
            dma((n_dp,)),
        ],
        compiler_params=pltpu.CompilerParams(collective_id=1, has_side_effects=True),
    )(rows, parcels)


def local(query_rows, key_rows, value_rows, grad_out, out_proj, lengths, offsets):
    data_ranks = lax.axis_size("dp")
    my_rank = lax.axis_index("dp")
    slot_count = offsets.shape[0]
    tokens_here = query_rows.shape[0]
    block_len = tokens_here // slot_count
    slot_ids = jnp.arange(slot_count, dtype=jnp.int32)
    peer_ids = jnp.arange(data_ranks, dtype=jnp.int32)
    targets = (my_rank + offsets) % data_ranks
    sources = (my_rank - offsets) % data_ranks
    home_lengths = lax.dynamic_slice_in_dim(lengths, my_rank * slot_count, slot_count, 0)
    segment, weight = doc_layout(home_lengths, block_len)
    weighted = (grad_out.astype(jnp.float32) * weight.reshape(-1, 1)).astype(jnp.bfloat16)
    group = HEADS // KVH
    features = query_rows.shape[1]
    kv_local = key_rows.shape[1] // HD

    line = lax.axis_size("mp")
    width = features * line
    gather = data_ranks * tokens_here * (features + width // data_ranks) < width * features
    piece = width // data_ranks
    fits = width % data_ranks == 0 and piece % 128 == 0 and features % piece == 0
    kernels = gather and fits and data_ranks % 2 == 0 and block_len % 16 == 0
    if kernels:
        whole_cot, cot_cols = spread(weighted, data_ranks, line)
        cot_cols = cot_cols.reshape(-1, piece)
    else:
        whole_cot = lax.all_gather(weighted, "mp", axis=1, tiled=True)
        if gather:
            cot_cols = lax.all_to_all(whole_cot, "dp", split_axis=1, concat_axis=0, tiled=True)
    head_grad = lax.dot_general(
        whole_cot, out_proj, (((1,), (1,)), ((), ())), preferred_element_type=jnp.float32
    ).astype(jnp.bfloat16)
    attended, grad_q, grad_k, grad_v = jax.vmap(block_grads)(
        query_rows.reshape(slot_count, block_len, kv_local, group, HD),
        key_rows.reshape(slot_count, block_len, kv_local, HD),
        value_rows.reshape(slot_count, block_len, kv_local, HD),
        head_grad.reshape(slot_count, block_len, kv_local, group, HD),
        segment,
    )
    attended_rows = attended.reshape(tokens_here, features)
    grads = jnp.concatenate(
        [part.reshape(slot_count, block_len, -1) for part in (grad_q, grad_k, grad_v)], axis=2
    )
    matches = targets[None, :] == peer_ids[:, None]
    picked = jnp.sum(jnp.where(matches, slot_ids[None, :], 0), axis=1)
    filled = jnp.any(matches, axis=1)
    parcels = jnp.where(filled[:, None, None], grads[picked], jnp.zeros((), grads.dtype))
    if kernels:
        everyone, arrived = share(attended_rows, parcels, data_ranks)
        everyone = everyone.reshape(-1, features)
    else:
        arrived = lax.all_to_all(parcels, "dp", split_axis=0, concat_axis=0, tiled=True)
    if gather:
        if not kernels:
            everyone = lax.all_gather(attended_rows, "dp", axis=0, tiled=True)
        grad_proj = lax.dot_general(
            cot_cols, everyone, (((0,), (0,)), ((), ())), preferred_element_type=jnp.float32
        )
    else:
        grad_proj = lax.psum_scatter(
            lax.dot_general(
                whole_cot, attended_rows, (((0,), (0,)), ((), ())), preferred_element_type=jnp.float32
            ),
            "dp",
            scatter_dimension=0,
            tiled=True,
        )
    moved = arrived[sources].reshape(tokens_here, -1)
    return (
        moved[:, :features],
        moved[:, features : features + key_rows.shape[1]],
        moved[:, features + key_rows.shape[1] :],
        grad_proj,
    )


def solution(mesh):
    return jax.shard_map(
        local,
        mesh=mesh,
        in_specs=(
            P("dp", "mp"),
            P("dp", "mp"),
            P("dp", "mp"),
            P("dp", "mp"),
            P("mp", None),
            P(),
            P(),
        ),
        out_specs=(P("dp", "mp"), P("dp", "mp"), P("dp", "mp"), P("dp", "mp")),
        check_vma=False,
    )
```

```python
import functools

import jax
import jax.numpy as jnp
from jax import lax
from jax.experimental import pallas as pl
from jax.experimental.pallas import tpu as pltpu
from jax.sharding import PartitionSpec as P

HEADS = 40
KVH = 8
HD = 128


def doc_layout(lengths, block_len):
    doc_ends = jnp.cumsum(lengths, axis=1)
    positions = jnp.arange(block_len, dtype=jnp.int32)
    segment = jnp.sum((doc_ends[:, None, :] <= positions[None, :, None]).astype(jnp.int32), axis=2)
    doc_ids = jnp.arange(lengths.shape[1], dtype=jnp.int32)
    onehot_doc = segment[:, :, None] == doc_ids[None, None, :]
    own_length = jnp.sum(jnp.where(onehot_doc, lengths[:, None, :], 0), axis=2)
    token_weight = 1.0 / own_length.astype(jnp.float32)
    return (segment, token_weight)


def block_grads(query_blk, key_blk, value_blk, grad_blk, segment):
    length = query_blk.shape[0]
    scaling = query_blk.shape[-1] ** (-0.5)
    positions = jnp.arange(length, dtype=jnp.int32)
    allowed = (segment[:, None] == segment[None, :]) & (positions[None, :] <= positions[:, None])
    scores = (
        jnp.einsum("qkgd,pkd->kgqp", query_blk, key_blk, preferred_element_type=jnp.float32)
        * scaling
    )
    scores = jnp.where(allowed[None, None], scores, -1e30)
    top_score = jnp.max(scores, axis=-1, keepdims=True)
    exponent = jnp.where(allowed[None, None], jnp.exp(scores - top_score), 0.0)
    denominator = jnp.sum(exponent, axis=-1, keepdims=True)
    soft = exponent / denominator
    soft_weight = soft.astype(jnp.bfloat16)
    attended = jnp.einsum(
        "kgqp,pkd->qkgd", soft_weight, value_blk, preferred_element_type=jnp.float32
    ).astype(jnp.bfloat16)
    row_dot = jnp.sum(grad_blk.astype(jnp.float32) * attended.astype(jnp.float32), axis=-1)
    grad_soft = jnp.einsum(
        "qkgd,pkd->kgqp", grad_blk, value_blk, preferred_element_type=jnp.float32
    )
    grad_score = (soft * (grad_soft - jnp.transpose(row_dot, (1, 2, 0))[..., None])).astype(
        jnp.bfloat16
    )
    grad_q = (
        jnp.einsum("kgqp,pkd->qkgd", grad_score, key_blk, preferred_element_type=jnp.float32)
        * scaling
    ).astype(jnp.bfloat16)
    grad_k = (
        jnp.einsum("kgqp,qkgd->pkd", grad_score, query_blk, preferred_element_type=jnp.float32)
        * scaling
    ).astype(jnp.bfloat16)
    grad_v = jnp.einsum(
        "kgqp,qkgd->pkd", soft_weight, grad_blk, preferred_element_type=jnp.float32
    ).astype(jnp.bfloat16)
    return (attended, grad_q, grad_k, grad_v)


def push(src, dst, send, recv, **where):
    return pltpu.make_async_remote_copy(
        src_ref=src,
        dst_ref=dst,
        send_sem=send,
        recv_sem=recv,
        device_id=where,
        device_id_type=pl.DeviceIdType.MESH,
    )


def greet(axis_sizes):
    barrier = pltpu.get_barrier_semaphore()
    for axis, size in axis_sizes:
        for step in range(1, size):
            pl.semaphore_signal(
                barrier,
                inc=1,
                device_id={axis: (lax.axis_index(axis) + step) % size},
                device_id_type=pl.DeviceIdType.MESH,
            )
    pl.semaphore_wait(barrier, sum(size - 1 for _, size in axis_sizes))


CHUNKS = 2


def spread_kernel(n_dp, n_mp, own, whole, cols, own_sem, z_send, z_recv, c_send, c_recv, c_own):
    d, m = lax.axis_index("dp"), lax.axis_index("mp")
    rows, feat = own.shape
    piece = cols.shape[2]
    per = feat // piece
    part = rows // CHUNKS

    def shard(j, c):
        return whole.at[pl.ds(c * part, part), pl.ds(pl.multiple_of(j * feat, 128), feat)]

    def hop(way, s, c):
        j = m - s if way == 0 else m + s
        src = own.at[pl.ds(c * part, part), :] if s == 0 else shard(j, c)
        goal = m + 1 if way == 0 else m - 1
        return push(src, shard(j, c), z_send.at[way, s, c], z_recv.at[way, s, c], mp=goal)

    def sends(way, s):
        return (m + 1 < n_mp) & (m - s >= 0) if way == 0 else (m >= 1) & (m + s < n_mp)

    def comes(way, s):
        return m - 1 - s >= 0 if way == 0 else m + 1 + s < n_mp

    def landing(way, s, c):
        j = m - 1 - s if way == 0 else m + 1 + s
        came = m - 1 if way == 0 else m + 1
        return push(shard(j, c), shard(j, c), z_send.at[way, s, c], z_recv.at[way, s, c], mp=came)

    def pass_columns(j, mine):
        for p in range(per):
            goal = j * per + p
            if mine:
                src = own.at[:, pl.ds(p * piece, piece)]
            else:
                src = whole.at[:, pl.ds(pl.multiple_of(j * feat + p * piece, 128), piece)]

            @pl.when(goal == d)
            def _():
                pltpu.make_async_copy(src, cols.at[d], c_own).start()

            @pl.when(goal != d)
            def _():
                push(src, cols.at[d], c_send.at[goal], c_recv.at[d], dp=goal).start()

    greet((("dp", n_dp), ("mp", n_mp)))
    for c in range(CHUNKS):
        for way in range(2):

            @pl.when(sends(way, 0))
            def _():
                hop(way, 0, c).start()

    keep = pltpu.make_async_copy(
        own, whole.at[:, pl.ds(pl.multiple_of(m * feat, 128), feat)], own_sem
    )
    keep.start()
    pass_columns(m, True)
    for s in range(n_mp - 1):
        for c in range(CHUNKS):
            for way in range(2):

                @pl.when(comes(way, s))
                def _():
                    landing(way, s, c).wait_recv()
                    if s + 1 < n_mp - 1:

                        @pl.when(sends(way, s + 1))
                        def _():
                            hop(way, s + 1, c).start()

        for way in range(2):

            @pl.when(comes(way, s))
            def _():
                pass_columns(m - 1 - s if way == 0 else m + 1 + s, False)

    keep.wait()
    for s in range(n_mp - 1):
        for c in range(CHUNKS):
            for way in range(2):

                @pl.when(sends(way, s))
                def _():
                    hop(way, s, c).wait_send()

    sample = own.at[:, pl.ds(0, piece)]
    pltpu.make_async_copy(sample, cols.at[d], c_own).wait()
    for peer in range(n_dp):

        @pl.when(peer != d)
        def _():
            copy = push(sample, cols.at[peer], c_send.at[peer], c_recv.at[peer], dp=peer)
            copy.wait_send()
            copy.wait_recv()


def share_kernel(
    n_dp, own, parcels, everyone, arrived, own_sem, a_send, a_recv, f_send, f_recv, p_send, p_recv, r_send, r_recv
):
    d = lax.axis_index("dp")
    chips = n_dp // 2
    chip, core = d // 2, d % 2
    mate = chip * 2 + 1 - core
    square = chips == 4
    half = own.shape[0] // 2

    def facing(k):
        if square:
            other = ((chip // 2) * 2 + 1 - chip % 2, (1 - chip // 2) * 2 + chip % 2, 3 - chip)[k - 1]
            return other, other
        return (chip + k) % chips, (chip + chips - k) % chips

    def relay(way, block_of, goal):
        part = everyone.at[block_of, pl.ds(way * half, half), :]
        return push(part, part, r_send.at[way], r_recv.at[way], dp=goal)

    greet((("dp", n_dp),))
    for k in range(1, 3 if square else chips):
        goal = facing(k)[0] * 2 + core
        push(own, everyone.at[d], a_send.at[k], a_recv.at[k], dp=goal).start()
    push(own, everyone.at[d], a_send.at[0], a_recv.at[0], dp=mate).start()
    for k in range(1, n_dp):
        goal = (d + k) % n_dp
        push(parcels.at[goal], arrived.at[d], p_send.at[k], p_recv.at[k], dp=goal).start()
    keeps = (
        pltpu.make_async_copy(own, everyone.at[d], own_sem.at[0]),
        pltpu.make_async_copy(parcels.at[d], arrived.at[d], own_sem.at[1]),
    )
    for keep in keeps:
        keep.start()

    def passed(k, side, goal):
        block = everyone.at[facing(k)[1] * 2 + side]
        return push(block, block, f_send.at[k], f_recv.at[k], dp=goal)

    for k in range(1, chips):
        origin = facing(k)[1] * 2 + core
        if square and k == 3:
            for way in range(2):
                relay(way, origin, facing(2 - way)[0] * 2 + core).wait_recv()
        else:
            push(own, everyone.at[origin], a_send.at[k], a_recv.at[k], dp=origin).wait_recv()
            if square:
                relay(k - 1, origin, facing(3 - k)[0] * 2 + core).start()
        passed(k, core, mate).start()
    push(own, everyone.at[mate], a_send.at[0], a_recv.at[0], dp=mate).wait_recv()
    for k in range(1, n_dp):
        origin = (d + n_dp - k) % n_dp
        copy = push(parcels.at[d], arrived.at[origin], p_send.at[k], p_recv.at[k], dp=origin)
        copy.wait_recv()
        copy.wait_send()
    for k in range(1, chips):
        passed(k, 1 - core, mate).wait_recv()
        passed(k, core, mate).wait_send()
    for k in range(3 if square else chips):
        push(own, everyone.at[d], a_send.at[k], a_recv.at[k], dp=mate).wait_send()
    if square:
        for way in range(2):
            relay(way, facing(way + 1)[1] * 2 + core, mate).wait_send()
    for keep in keeps:
        keep.wait()


def spread(weighted, n_dp, n_mp):
    rows, feat = weighted.shape
    piece = feat * n_mp // n_dp
    dma = pltpu.SemaphoreType.DMA
    anywhere = pl.BlockSpec(memory_space=pl.ANY)
    return pl.pallas_call(
        functools.partial(spread_kernel, n_dp, n_mp),
        out_shape=(
            jax.ShapeDtypeStruct((rows, feat * n_mp), weighted.dtype),
            jax.ShapeDtypeStruct((n_dp, rows, piece), weighted.dtype),
        ),
        in_specs=[anywhere],
        out_specs=(anywhere, anywhere),
        scratch_shapes=[
            dma(()),
            dma((2, n_mp - 1, CHUNKS)),
            dma((2, n_mp - 1, CHUNKS)),
            dma((n_dp,)),
            dma((n_dp,)),
            dma(()),
        ],
        compiler_params=pltpu.CompilerParams(collective_id=0, has_side_effects=True),
    )(weighted)


def share(rows, parcels, n_dp):
    dma = pltpu.SemaphoreType.DMA
    anywhere = pl.BlockSpec(memory_space=pl.ANY)
    return pl.pallas_call(
        functools.partial(share_kernel, n_dp),
        out_shape=(
            jax.ShapeDtypeStruct((n_dp, *rows.shape), rows.dtype),
            jax.ShapeDtypeStruct(parcels.shape, parcels.dtype),
        ),
        in_specs=[anywhere, anywhere],
        out_specs=(anywhere, anywhere),
        scratch_shapes=[
            dma((2,)),
            dma((n_dp // 2,)),
            dma((n_dp // 2,)),
            dma((n_dp // 2,)),
            dma((n_dp // 2,)),
            dma((n_dp,)),
            dma((n_dp,)),
            dma((2,)),
            dma((2,)),
        ],
        compiler_params=pltpu.CompilerParams(collective_id=1, has_side_effects=True),
    )(rows, parcels)


def local(query_rows, key_rows, value_rows, grad_out, out_proj, lengths, offsets):
    data_ranks = lax.axis_size("dp")
    my_rank = lax.axis_index("dp")
    slot_count = offsets.shape[0]
    tokens_here = query_rows.shape[0]
    block_len = tokens_here // slot_count
    slot_ids = jnp.arange(slot_count, dtype=jnp.int32)
    peer_ids = jnp.arange(data_ranks, dtype=jnp.int32)
    targets = (my_rank + offsets) % data_ranks
    sources = (my_rank - offsets) % data_ranks
    home_lengths = lax.dynamic_slice_in_dim(lengths, my_rank * slot_count, slot_count, 0)
    segment, weight = doc_layout(home_lengths, block_len)
    weighted = (grad_out.astype(jnp.float32) * weight.reshape(-1, 1)).astype(jnp.bfloat16)
    group = HEADS // KVH
    features = query_rows.shape[1]
    kv_local = key_rows.shape[1] // HD

    line = lax.axis_size("mp")
    width = features * line
    gather = data_ranks * tokens_here * (features + width // data_ranks) < width * features
    piece = width // data_ranks
    fits = width % data_ranks == 0 and piece % 128 == 0 and features % piece == 0
    kernels = gather and fits and data_ranks % 2 == 0 and block_len % 16 == 0 and tokens_here % 32 == 0
    if kernels:
        whole_cot, cot_cols = spread(weighted, data_ranks, line)
        cot_cols = cot_cols.reshape(-1, piece)
    else:
        whole_cot = lax.all_gather(weighted, "mp", axis=1, tiled=True)
        if gather:
            cot_cols = lax.all_to_all(whole_cot, "dp", split_axis=1, concat_axis=0, tiled=True)
    head_grad = lax.dot_general(
        whole_cot, out_proj, (((1,), (1,)), ((), ())), preferred_element_type=jnp.float32
    ).astype(jnp.bfloat16)
    attended, grad_q, grad_k, grad_v = jax.vmap(block_grads)(
        query_rows.reshape(slot_count, block_len, kv_local, group, HD),
        key_rows.reshape(slot_count, block_len, kv_local, HD),
        value_rows.reshape(slot_count, block_len, kv_local, HD),
        head_grad.reshape(slot_count, block_len, kv_local, group, HD),
        segment,
    )
    attended_rows = attended.reshape(tokens_here, features)
    grads = jnp.concatenate(
        [part.reshape(slot_count, block_len, -1) for part in (grad_q, grad_k, grad_v)], axis=2
    )
    matches = targets[None, :] == peer_ids[:, None]
    picked = jnp.sum(jnp.where(matches, slot_ids[None, :], 0), axis=1)
    filled = jnp.any(matches, axis=1)
    parcels = jnp.where(filled[:, None, None], grads[picked], jnp.zeros((), grads.dtype))
    if kernels:
        everyone, arrived = share(attended_rows, parcels, data_ranks)
        everyone = everyone.reshape(-1, features)
    else:
        arrived = lax.all_to_all(parcels, "dp", split_axis=0, concat_axis=0, tiled=True)
    if gather:
        if not kernels:
            everyone = lax.all_gather(attended_rows, "dp", axis=0, tiled=True)
        grad_proj = lax.dot_general(
            cot_cols, everyone, (((0,), (0,)), ((), ())), preferred_element_type=jnp.float32
        )
    else:
        grad_proj = lax.psum_scatter(
            lax.dot_general(
                whole_cot, attended_rows, (((0,), (0,)), ((), ())), preferred_element_type=jnp.float32
            ),
            "dp",
            scatter_dimension=0,
            tiled=True,
        )
    moved = arrived[sources].reshape(tokens_here, -1)
    return (
        moved[:, :features],
        moved[:, features : features + key_rows.shape[1]],
        moved[:, features + key_rows.shape[1] :],
        grad_proj,
    )


def solution(mesh):
    return jax.shard_map(
        local,
        mesh=mesh,
        in_specs=(
            P("dp", "mp"),
            P("dp", "mp"),
            P("dp", "mp"),
            P("dp", "mp"),
            P("mp", None),
            P(),
            P(),
        ),
        out_specs=(P("dp", "mp"), P("dp", "mp"), P("dp", "mp"), P("dp", "mp")),
        check_vma=False,
    )
```
